32 devices in a mesh: rep: 16 (over z, y, core), tp: 2 (over x).
Axes of the slice: x: 2, y: 2, z: 4, core: 2. Of those that a mesh axis runs over, the one named last changes fastest.
Arguments:
- acts: bfloat16 [16, 256, 4096], P('rep', 'tp'), may hold values from -6 to 6
- weights: bfloat16 [16, 4096, 4096], P('rep', None, 'tp'), may hold values from -6 to 6
- cotangent: bfloat16 [16, 256, 4096], P('rep', None, 'tp'), may hold values from -6 to 6
- start_factors: float32 [4096, 32], replicated, may hold values from -6 to 6
Outputs:
- projected: bfloat16 [16, 256, 4096], P('rep', None, 'tp')
- new_weights: bfloat16 [16, 4096, 4096], P('rep', None, 'tp')
The draws below stay inside these ranges and needn't reach their ends.
All inputs are finite; a program needn't handle non-finite values.
Results may differ from the reference program's by a relative error of at most 0.001.
Values may be sent and summed in bfloat16 or wider, within the bound.
A program may use at most 128 MiB of HBM per device.

```python
import jax
import jax.numpy as jnp
from jax import lax

D = 4096
R = 32
STEPS = 3
TOKENS = 256
REPS = 16


def block_scale(rng, extent, split, least, top_value):
    def one(dim, blocks):
        heights = jax.random.uniform(jax.random.fold_in(jax.random.fold_in(rng, 6), dim), (blocks,), jnp.float32, least / len(split), top_value / len(split))
        return jnp.repeat(jnp.exp(heights), extent[dim] // blocks).reshape((-1,) + (1,) * (len(extent) - dim - 1))

    loudness = one(*split[0])
    for cut in split[1:]:
        loudness = loudness * one(*cut)
    return loudness


def normal_values(own_key, dims, width, bound, pieces=(), kind=jnp.bfloat16):
    loudness = block_scale(own_key, dims, pieces, -0.22, 0.18) if pieces else 1.0
    result = jax.random.normal(own_key, dims, jnp.float32) * width * loudness
    return jnp.minimum(jnp.maximum(result, -bound), bound).astype(kind)


def setup_inputs(seed: int = 0) -> dict:
    streams_of = jax.random.split(jax.random.key(seed), 5)
    acts = normal_values(streams_of[0], (REPS, TOKENS, D), 1.0, 6.0, ((0, 16), (1, 2)))
    weights = normal_values(streams_of[1], (REPS, D, D), 1.0, 6.0, ((0, 16), (2, 2)))
    cotangent = normal_values(streams_of[2], (REPS, TOKENS, D), 1.0, 6.0, ((0, 16), (2, 2)))
    start_factors = normal_values(streams_of[3], (D, R), 1.0, 6.0, (), jnp.float32)
    return dict(acts=acts, weights=weights, cotangent=cotangent, start_factors=start_factors)


HIGH = lax.Precision.HIGHEST

def reference(acts, weights, cotangent, start_factors):
    scale = D ** (-0.5)

    def forward(pair):
        return (jnp.dot(pair[0].astype(jnp.float32), pair[1].astype(jnp.float32), preferred_element_type=jnp.float32) * scale).astype(jnp.bfloat16)
    projected = lax.map(forward, (acts, weights))

    def stepped(triple):
        grad = lax.dot_general(triple[0].astype(jnp.float32), triple[2].astype(jnp.float32), (((0,), (0,)), ((), ())), preferred_element_type=jnp.float32)
        return triple[1].astype(jnp.float32) - 0.5 * scale * grad
    current = lax.map(stepped, (acts, weights, cotangent))
    index = jnp.arange(REPS, dtype=jnp.int32)
    for step in range(STEPS):
        partner = jnp.bitwise_xor(index, jnp.int32(1 << step))
        side = jnp.einsum('rio,ik->rok', current, start_factors, precision=HIGH)
        diff = side - side[partner]
        gram = jnp.einsum('rok,rol->rkl', diff, diff, precision=HIGH)
        lower = jnp.linalg.cholesky(gram)
        solved = jax.scipy.linalg.solve_triangular(lower, jnp.transpose(diff, (0, 2, 1)), lower=True)
        ortho = jnp.transpose(solved, (0, 2, 1))
        local = jnp.einsum('rio,rok->rik', current, ortho, precision=HIGH)
        back = local + local[partner]
        current = current - 0.5 * jnp.einsum('rik,rok->rio', back, ortho, precision=HIGH)
    return (projected, current.astype(jnp.bfloat16))
```

```python
import jax
import jax.numpy as jnp
from jax import lax
from jax.sharding import PartitionSpec as P

STEPS = 3
F32, BF16, F16 = jnp.float32, jnp.bfloat16, jnp.float16
HIGH = lax.Precision.HIGHEST


def partner(block, axis, stride):
    count = lax.axis_size(axis)
    route = [(low, low ^ (1 << stride)) for low in range(count)]
    return lax.ppermute(block, axis, route)


def split(x, terms):
    out = []
    for _ in range(terms):
        part = lax.reduce_precision(x, 8, 7)
        out.append(part.astype(BF16))
        x = x - part
    return out


def dot(a, b, ca, cb):
    return lax.dot_general(a, b, (((ca,), (cb,)), ((), ())), preferred_element_type=F32)


def folded(out, terms):
    return out.reshape((terms, -1) + out.shape[1:]).sum(0)


def gather(x, axis):
    n = lax.axis_size("tp")
    if n != 2:
        return lax.all_gather(x, "tp", axis=axis, tiled=True)
    me = lax.axis_index("tp")
    other = partner(x, "tp", 0)
    size = x.shape[axis]
    shape = list(x.shape)
    shape[axis] = 2 * size
    full = jnp.zeros(shape, x.dtype)
    full = lax.dynamic_update_slice_in_dim(full, x, me * size, axis)
    return lax.dynamic_update_slice_in_dim(full, other, (1 - me) * size, axis)


def total(x):
    if lax.axis_size("tp") != 2:
        return lax.psum(x, "tp")
    return x + partner(x, "tp", 0)


def scattered(x):
    n = lax.axis_size("tp")
    if n != 2:
        return lax.psum_scatter(x, "tp", scatter_dimension=1, tiled=True)
    me = lax.axis_index("tp")
    size = x.shape[1] // 2
    mine = lax.dynamic_slice_in_dim(x, me * size, size, 1)
    theirs = lax.dynamic_slice_in_dim(x, (1 - me) * size, size, 1)
    return mine + partner(theirs.astype(F16), "tp", 0).astype(F32)


def shards(acts, weights, cotangent, start_factors):
    d, rank = start_factors.shape
    scale = d ** (-0.5)
    mine, w, c = acts[0], weights[0], cotangent[0]

    full = gather(mine, 0)
    s3 = jnp.concatenate(split(start_factors.T, 3), 0)
    acts_s = gather(folded(dot(s3, mine, 1, 1), 3), 1)
    side = folded(dot(s3, w, 1, 0), 3)
    a3 = jnp.concatenate(split(acts_s, 3), 0)
    side = side - 0.5 * scale * folded(dot(a3, c, 1, 0), 3)

    diffs = []
    for step in range(STEPS):
        other = partner(side, "rep", step)
        diffs.append(side - other)
        side = 0.5 * (side + other)
    diff = jnp.concatenate(diffs, 0)
    gram = total(lax.dot_general(diff, diff, (((1,), (1,)), ((), ())), precision=HIGH))
    blocks = gram.reshape(STEPS, rank, STEPS, rank)
    lower = jnp.linalg.cholesky(jnp.stack([blocks[s, :, s] for s in range(STEPS)]))
    eye = jnp.broadcast_to(jnp.eye(rank, dtype=F32), lower.shape)
    inv = lax.linalg.triangular_solve(lower, eye, left_side=True, lower=True)
    ortho = jnp.einsum("skl,slo->sko", inv, diff.reshape(STEPS, rank, -1), precision=HIGH)
    ortho = ortho.reshape(STEPS * rank, -1)
    cross = {}
    for s in range(STEPS):
        for t in range(s):
            half = jnp.dot(inv[s], blocks[s, :, t], precision=HIGH)
            cross[s, t] = jnp.dot(half, inv[t].T, precision=HIGH)

    o_hi, o_lo = split(ortho, 2)
    o2 = jnp.concatenate([o_hi, o_lo], 0)
    co = folded(dot(o2, c, 1, 1), 2)
    co2 = jnp.concatenate(split(co, 2), 0)
    x = folded(dot(o2, w, 1, 1) - 0.5 * scale * dot(co2, full, 1, 0), 2)

    backs = []
    for step in range(STEPS):
        local = scattered(x[step * rank:(step + 1) * rank])
        for t in range(step):
            local = local - 0.5 * jnp.dot(cross[step, t], backs[t], precision=HIGH)
        if step == 0:
            other = partner(local, "rep", step)
        else:
            other = partner(local.astype(F16), "rep", step).astype(F32)
        backs.append(local + other)
    back = jnp.concatenate([gather(b.astype(F16), 1).astype(F32) for b in backs], 0)

    projected = (dot(full, w, 1, 0) * scale).astype(BF16)[None]
    b_hi, b_lo = split(-0.5 * back, 2)
    left = jnp.concatenate([full * jnp.asarray(-0.5 * scale, BF16), b_hi, b_hi, b_lo], 0)
    right = jnp.concatenate([c, o_hi, o_lo, o_hi], 0)
    new = (w.astype(F32) + dot(left, right, 0, 0)).astype(BF16)[None]
    return projected, new


def solution(mesh):
    in_specs = (P("rep", "tp", None), P("rep", None, "tp"), P("rep", None, "tp"), P())
    out_specs = (P("rep", None, "tp"), P("rep", None, "tp"))
    return jax.shard_map(shards, mesh=mesh, in_specs=in_specs, out_specs=out_specs, check_vma=False)
```

```python
import functools

import jax
import jax.numpy as jnp
from jax import lax
from jax.experimental import pallas as pl
from jax.experimental.pallas import tpu as pltpu
from jax.sharding import PartitionSpec as P

STEPS = 3
F32, BF16, F16 = jnp.float32, jnp.bfloat16, jnp.float16
HIGH = lax.Precision.HIGHEST


def partner(block, axis, stride):
    count = lax.axis_size(axis)
    route = [(low, low ^ (1 << stride)) for low in range(count)]
    return lax.ppermute(block, axis, route)


def split(x, terms):
    out = []
    for _ in range(terms):
        part = lax.reduce_precision(x, 8, 7)
        out.append(part.astype(BF16))
        x = x - part
    return out


def dot(a, b, ca, cb):
    return lax.dot_general(a, b, (((ca,), (cb,)), ((), ())), preferred_element_type=F32)


def folded(out, terms):
    return out.reshape((terms, -1) + out.shape[1:]).sum(0)


def gather(x, axis):
    n = lax.axis_size("tp")
    if n != 2:
        return lax.all_gather(x, "tp", axis=axis, tiled=True)
    me = lax.axis_index("tp")
    other = partner(x, "tp", 0)
    size = x.shape[axis]
    shape = list(x.shape)
    shape[axis] = 2 * size
    full = jnp.zeros(shape, x.dtype)
    full = lax.dynamic_update_slice_in_dim(full, x, me * size, axis)
    return lax.dynamic_update_slice_in_dim(full, other, (1 - me) * size, axis)


def total(x):
    if lax.axis_size("tp") != 2:
        return lax.psum(x, "tp")
    return x + partner(x, "tp", 0)


def scattered(x):
    n = lax.axis_size("tp")
    if n != 2:
        return lax.psum_scatter(x, "tp", scatter_dimension=1, tiled=True)
    me = lax.axis_index("tp")
    size = x.shape[1] // 2
    mine = lax.dynamic_slice_in_dim(x, me * size, size, 1)
    theirs = lax.dynamic_slice_in_dim(x, (1 - me) * size, size, 1)
    return mine + partner(theirs.astype(F16), "tp", 0).astype(F32)


def parts(x):
    high = x.astype(BF16)
    return high, (x - high.astype(F32)).astype(BF16)


def limits(mib):
    return pltpu.CompilerParams(vmem_limit_bytes=mib * 1024 * 1024)


def factor_kernel(rank, gram_ref, diff_ref, o_ref, cross_ref):
    row = lax.broadcasted_iota(jnp.int32, (rank, rank), 0)
    col = lax.broadcasted_iota(jnp.int32, (rank, rank), 1)
    unit = (row == col).astype(F32)
    gram = [[gram_ref[s * rank:(s + 1) * rank, t * rank:(t + 1) * rank] for t in range(s + 1)] for s in range(STEPS)]
    rest = [gram[s][s] for s in range(STEPS)]
    inv = [unit] * STEPS
    for k in range(rank - 1):
        for s in range(STEPS):
            pivot = rest[s][k:k + 1, :]
            ratio = rest[s][:, k:k + 1] / pivot[:, k:k + 1]
            ratio = jnp.where(row > k, jnp.broadcast_to(ratio, (rank, rank)), 0.0)
            inv[s] = inv[s] - ratio * inv[s][k:k + 1, :]
            rest[s] = rest[s] - ratio * pivot
    for s in range(STEPS):
        pivots = jnp.sum(rest[s] * unit, axis=1, keepdims=True)
        inv[s] = inv[s] / jnp.sqrt(pivots)
        rows = pl.ds(s * rank, rank)
        ortho = jnp.dot(inv[s], diff_ref[rows, :], precision=HIGH, preferred_element_type=F32)
        high, low = parts(ortho)
        o_ref[rows, :] = high
        o_ref[pl.ds((STEPS + s) * rank, rank), :] = low
        o_ref[pl.ds((2 * STEPS + s) * rank, rank), :] = high
        for t in range(STEPS):
            if t < s:
                half = jnp.dot(inv[s], gram[s][t], precision=HIGH, preferred_element_type=F32)
                cross_ref[s, t] = lax.dot_general(
                    half, inv[t], (((1,), (1,)), ((), ())), precision=HIGH, preferred_element_type=F32)
            else:
                cross_ref[s, t] = jnp.zeros((rank, rank), F32)


def input_kernel(count, factor, o_ref, c_ref, full_ref, w_ref, x_ref, co_ref):
    @pl.when(pl.program_id(0) == 0)
    def _():
        both = dot(o_ref[...], c_ref[...], 1, 1)
        high, low = parts(both[:count] + both[count:])
        co_ref[:count, :] = high
        co_ref[count:, :] = low

    both = dot(o_ref[...], w_ref[...], 1, 1) - factor * dot(co_ref[...], full_ref[...], 1, 0)
    x_ref[...] = both[:count] + both[count:]


def update_kernel(factor, full_ref, b_ref, c_ref, o_ref, w_ref, new_ref):
    high, low = parts(-0.5 * b_ref[...])
    left = jnp.concatenate([high, high, low], 0)
    change = dot(full_ref[...] * jnp.asarray(-factor, BF16), c_ref[...], 0, 0) + dot(left, o_ref[...], 0, 0)
    new_ref[...] = (w_ref[...].astype(F32) + change).astype(BF16)


def shards(acts, weights, cotangent, start_factors):
    d, rank = start_factors.shape
    scale = d ** (-0.5)
    mine, w, c = acts[0], weights[0], cotangent[0]

    full = gather(mine, 0)
    s3 = jnp.concatenate(split(start_factors.T, 3), 0)
    acts_s = gather(folded(dot(s3, mine, 1, 1), 3), 1)
    side = folded(dot(s3, w, 1, 0), 3)
    a3 = jnp.concatenate(split(acts_s, 3), 0)
    side = side - 0.5 * scale * folded(dot(a3, c, 1, 0), 3)

    diffs = []
    for step in range(STEPS):
        other = partner(side, "rep", step)
        diffs.append(side - other)
        side = 0.5 * (side + other)
    diff = jnp.concatenate(diffs, 0)
    gram = total(lax.dot_general(diff, diff, (((1,), (1,)), ((), ())), precision=HIGH))
    count = STEPS * rank
    width, tokens = w.shape[1], full.shape[0]
    o3, cross = pl.pallas_call(
        functools.partial(factor_kernel, rank),
        out_shape=(jax.ShapeDtypeStruct((3 * count, width), BF16), jax.ShapeDtypeStruct((STEPS, STEPS, rank, rank), F32)),
        compiler_params=limits(16),
        name="factor",
    )(gram, diff)

    tile = 512
    x = pl.pallas_call(
        functools.partial(input_kernel, count, 0.5 * scale),
        grid=(d // tile,),
        in_specs=[
            pl.BlockSpec((2 * count, width), lambda i: (0, 0)),
            pl.BlockSpec((tokens, width), lambda i: (0, 0)),
            pl.BlockSpec((tokens, tile), lambda i: (0, i)),
            pl.BlockSpec((tile, width), lambda i: (i, 0)),
        ],
        out_specs=pl.BlockSpec((count, tile), lambda i: (0, i)),
        out_shape=jax.ShapeDtypeStruct((count, d), F32),
        scratch_shapes=[pltpu.VMEM((2 * count, tokens), BF16)],
        compiler_params=limits(24),
        name="input_side",
    )(o3, c, full, w)
    backs = []
    for step in range(STEPS):
        local = scattered(x[step * rank:(step + 1) * rank])
        for t in range(step):
            local = local - 0.5 * jnp.dot(cross[step, t], backs[t], precision=HIGH)
        if step == 0:
            other = partner(local, "rep", step)
        else:
            other = partner(local.astype(F16), "rep", step).astype(F32)
        backs.append(local + other)
        if step == 0:
            late, backs[0] = lax.optimization_barrier((full, backs[0]))
    back = jnp.concatenate([gather(b.astype(F16), 1).astype(F32) for b in backs], 0)

    projected = (dot(late, w, 1, 0) * scale).astype(BF16)[None]
    tile = 256
    new = pl.pallas_call(
        functools.partial(update_kernel, 0.5 * scale),
        grid=(d // tile,),
        in_specs=[
            pl.BlockSpec((tokens, tile), lambda i: (0, i)),
            pl.BlockSpec((count, tile), lambda i: (0, i)),
            pl.BlockSpec((tokens, width), lambda i: (0, 0)),
            pl.BlockSpec((3 * count, width), lambda i: (0, 0)),
            pl.BlockSpec((tile, width), lambda i: (i, 0)),
        ],
        out_specs=pl.BlockSpec((tile, width), lambda i: (i, 0)),
        out_shape=jax.ShapeDtypeStruct(w.shape, BF16),
        compiler_params=limits(24),
        name="update",
    )(full, back, c, o3, w)[None]
    return projected, new


def solution(mesh):
    in_specs = (P("rep", "tp", None), P("rep", None, "tp"), P("rep", None, "tp"), P())
    out_specs = (P("rep", None, "tp"), P("rep", None, "tp"))
    return jax.shard_map(shards, mesh=mesh, in_specs=in_specs, out_specs=out_specs, check_vma=False)
```
